32 devices in a mesh: blade: 16 (over z, y, x), inst: 2 (over core).
Axes of the slice: x: 2, y: 2, z: 4, core: 2. Of those that a mesh axis runs over, the one named last changes fastest.
Arguments:
- tangent_seed: float32 [16, 5, 24, 1024], P('blade', None, 'inst'), may hold values from -6 to 6
- adjoint_seed: float32 [16, 5, 24, 1024], P('blade', None, 'inst'), may hold values from -6 to 6
- jacobian: bfloat16 [16, 24, 25, 1024], P('blade', 'inst'), may hold values from -1 to 4
- precond: bfloat16 [16, 24, 25, 1024], P('blade', 'inst'), may hold values from -1 to 4
- upwind: float32 [16, 1024], P('blade'), may hold values from 0.2 to 1
- up_weight: float32 [16, 256], P('blade'), may hold values from 0.3 to 1.2
- bottom_face_strength: float32 [16, 256], P('blade'), may hold values from 0.3 to 1.2
- up_cells: int32 [256], replicated, may hold values from 0 to 1023, as said below
- lo_cells: int32 [256], replicated, may hold values from 0 to 1023, as said below
- phase_index: int32 [11], replicated, may hold values from 0 to 15
Outputs:
- tangent_out: float32 [16, 5, 24, 1024], P('blade', None, 'inst')
- adjoint_out: float32 [16, 5, 24, 1024], P('blade', None, 'inst')
The draws below stay inside these ranges and needn't reach their ends.
Inputs may be any that keep to these rules, and one draw needn't show every extreme that they name: `up_cells`: entry f of the table is one of the cells 4 f to 4 f + 3. `lo_cells`: entry f of the table is one of the cells 4 f to 4 f + 3.
All inputs are finite; a program needn't handle non-finite values.
Results may differ from the reference program's by a relative error of at most 0.0003.
Values sent between devices are 32-bit elements; how exact they have to be, the bound alone decides.
A program may use at most 64 MiB of HBM per device.

```python
import math
import jax
import jax.numpy as jnp
from jax import lax

CELLS = 1024
SNAPSHOT_COUNT = 24
NV = 5
NH = 11
FACE = 256
P_SIZE = 16


def block_law(key):
    key_diag, key_off = jax.random.split(key)
    full_shape = (P_SIZE, SNAPSHOT_COUNT, NV, NV, CELLS)
    equation_slot_number = lax.broadcasted_iota(jnp.int32, full_shape, 2)
    column_position_index = lax.broadcasted_iota(jnp.int32, full_shape, 3)
    identity_mask = (equation_slot_number == column_position_index).astype(jnp.float32)
    diagonal = jnp.exp(jax.random.uniform(key_diag, full_shape, jnp.float32, math.log(1.5), math.log(4.0)))
    coupling = jnp.clip(0.3 * jax.random.normal(key_off, full_shape, jnp.float32), -1.0, 1.0)
    blocks = identity_mask * diagonal + (1.0 - identity_mask) * coupling
    return blocks.reshape((P_SIZE, SNAPSHOT_COUNT, NV * NV, CELLS))


def draw_jacobian(key, part):
    return block_law(jax.random.fold_in(key, 11)).astype(jnp.bfloat16)


def draw_precond(key, part):
    return block_law(jax.random.fold_in(key, 23)).astype(jnp.bfloat16)


def face_table(key):
    within = jax.random.randint(key, (FACE,), 0, 4).astype(jnp.int32)
    within = within.at[0].set(0).at[FACE - 1].set(3)
    return jnp.arange(FACE, dtype=jnp.int32) * 4 + within


def draw_up_cells(key, part):
    return face_table(jax.random.fold_in(key, 5))


def draw_lo_cells(key, part):
    return face_table(jax.random.fold_in(key, 7))


def draw_phase_index(key, part):
    random_generator_seed, key_high, key_low = jax.random.split(jax.random.fold_in(key, 3), 3)
    slot_numbers = jax.random.randint(random_generator_seed, (NH,), 0, P_SIZE).astype(jnp.int32)
    high_slot = jax.random.randint(key_high, (), 0, NH).astype(jnp.int32)
    low_slot = jnp.mod(high_slot + 1 + jax.random.randint(key_low, (), 0, NH - 1).astype(jnp.int32), NH)
    return slot_numbers.at[high_slot].set(P_SIZE - 1).at[low_slot].set(0)


def block_levels(stream_key, shape, cuts, least, top_value):
    level, own = 1.0, jax.random.fold_in(stream_key, 6)
    for position, shards_of in cuts:
        draws = jnp.exp(jax.random.uniform(jax.random.fold_in(own, position), (shards_of,), jnp.float32, least / len(cuts), top_value / len(cuts)))
        level = level * jnp.repeat(draws, shape[position] // shards_of).reshape([-1 if axis == position else 1 for axis in range(len(shape))])
    return level


def bell_draw(stream_key, shape, spread, limit, pieces=(), kind=jnp.bfloat16):
    result = jax.random.normal(stream_key, shape, jnp.float32) * spread
    if len(pieces) > 0:
        result = block_levels(stream_key, shape, pieces, -0.22, 0.18) * result
    return jnp.clip(result, min=-limit, max=limit).astype(kind)


def setup_inputs(seed: int = 0) -> dict:
    keys = jax.random.split(jax.random.key(seed), 11)
    tangent_seed = bell_draw(keys[0], (P_SIZE, NV, SNAPSHOT_COUNT, CELLS), 1.0, 6.0, ((0, 16), (2, 2)), jnp.float32)
    adjoint_seed = bell_draw(keys[1], (P_SIZE, NV, SNAPSHOT_COUNT, CELLS), 1.0, 6.0, ((0, 16), (2, 2)), jnp.float32)
    jacobian = draw_jacobian(jax.random.fold_in(keys[10], 71), 0)
    precond = draw_precond(jax.random.fold_in(keys[10], 71), 0)
    upwind = jnp.clip(jnp.exp(math.log(1.0) - 1.609438 * jax.random.uniform(keys[4], (P_SIZE, CELLS), jnp.float32) ** block_levels(keys[4], (P_SIZE, CELLS), ((0, 16),), -0.2, 0.2)), 0.2, 1.0)
    up_weight = jnp.clip(jnp.exp(math.log(1.2) - 1.3862944 * jax.random.uniform(keys[5], (P_SIZE, FACE), jnp.float32) ** block_levels(keys[5], (P_SIZE, FACE), ((0, 16),), -0.2, 0.2)), 0.3, 1.2)
    bottom_face_strength = jnp.clip(jnp.exp(math.log(1.2) - 1.3862944 * jax.random.uniform(keys[6], (P_SIZE, FACE), jnp.float32) ** block_levels(keys[6], (P_SIZE, FACE), ((0, 16),), -0.2, 0.2)), 0.3, 1.2)
    up_cells = draw_up_cells(jax.random.fold_in(keys[10], 71), 0)
    lo_cells = draw_lo_cells(jax.random.fold_in(keys[10], 71), 0)
    phase_index = draw_phase_index(jax.random.fold_in(keys[10], 71), 0)
    return {"tangent_seed": tangent_seed, "adjoint_seed": adjoint_seed, "jacobian": jacobian, "precond": precond, "upwind": upwind, "up_weight": up_weight, "bottom_face_strength": bottom_face_strength, "up_cells": up_cells, "lo_cells": lo_cells, "phase_index": phase_index}


OMEGA = 0.15


def spectral(phase_index, passages):
    sampled_moments = jnp.arange(SNAPSHOT_COUNT, dtype=jnp.int32)
    snapshot_displacement = sampled_moments[:, None] - sampled_moments[None, :]
    orders = jnp.arange(1, NH + 1, dtype=jnp.int32)
    wrapped = jnp.mod(orders[:, None, None] * snapshot_displacement[None, :, :], SNAPSHOT_COUNT).astype(jnp.float32) / SNAPSHOT_COUNT
    weights = orders.astype(jnp.float32)[:, None, None]
    skewed = -(2.0 / SNAPSHOT_COUNT) * jnp.sum(weights * jnp.sin(2.0 * jnp.pi * wrapped), axis=0)
    derivative = 0.5 * skewed - 0.5 * skewed.T
    phase_angle = phase_index.astype(jnp.float32)[:, None, None] / passages
    parity = 1.0 - 2.0 * jnp.mod(snapshot_displacement, 2).astype(jnp.float32)
    rotation = (1.0 + parity) / SNAPSHOT_COUNT + (2.0 / SNAPSHOT_COUNT) * jnp.sum(jnp.cos(2.0 * jnp.pi * (wrapped - phase_angle)), axis=0)
    return derivative, rotation


def block_apply(blocks, vector):
    variables = vector.shape[1]
    result_rows = []
    for row_index in range(variables):
        summed = blocks[:, :, row_index * variables, :] * vector[:, 0]
        for column_index in range(1, variables):
            summed = summed + blocks[:, :, row_index * variables + column_index, :] * vector[:, column_index]
        result_rows.append(summed)
    return jnp.stack(result_rows, axis=1)


def block_apply_t(blocks, vector):
    variables = vector.shape[1]
    result_rows = []
    for column_index in range(variables):
        summed = blocks[:, :, column_index, :] * vector[:, 0]
        for row_index in range(1, variables):
            summed = summed + blocks[:, :, row_index * variables + column_index, :] * vector[:, row_index]
        result_rows.append(summed)
    return jnp.stack(result_rows, axis=1)


def instance_mix(matrix, vector):
    return jnp.einsum('ts,pvsc->pvtc', matrix, vector, precision=lax.Precision.HIGHEST)


def reference(tangent_seed, adjoint_seed, jacobian, precond, upwind, up_weight, bottom_face_strength, up_cells, lo_cells, phase_index):
    derivative, rotation = spectral(phase_index, P_SIZE)
    padding = ((0, 0), (0, 0), (0, 0), (1, 0))
    rot_lo = instance_mix(rotation, tangent_seed[..., lo_cells])
    rot_up = instance_mix(rotation.T, tangent_seed[..., up_cells])
    shifted = jnp.pad(tangent_seed[..., :-1], padding)
    applied = block_apply(jacobian, tangent_seed) - upwind[:, None, None, :] * shifted + OMEGA * instance_mix(derivative, tangent_seed)
    applied = applied.at[..., up_cells].add(-up_weight[:, None, None, :] * jnp.roll(rot_lo, -1, axis=0))
    applied = applied.at[..., lo_cells].add(-bottom_face_strength[:, None, None, :] * jnp.roll(rot_up, 1, axis=0))
    tangent_out = block_apply(precond, applied)
    dual_field = block_apply_t(precond, adjoint_seed)
    rot_lo = instance_mix(rotation, dual_field[..., lo_cells])
    rot_up = instance_mix(rotation.T, dual_field[..., up_cells])
    shifted = jnp.pad((upwind[:, None, None, :] * dual_field)[..., 1:], ((0, 0), (0, 0), (0, 0), (0, 1)))
    adjoint_out = block_apply_t(jacobian, dual_field) - shifted + OMEGA * instance_mix(derivative.T, dual_field)
    adjoint_out = adjoint_out.at[..., lo_cells].add(-jnp.roll(up_weight[:, None, None, :] * rot_up, 1, axis=0))
    adjoint_out = adjoint_out.at[..., up_cells].add(-jnp.roll(bottom_face_strength[:, None, None, :] * rot_lo, -1, axis=0))
    return tangent_out, adjoint_out
```

```python
import functools
import math

import jax
import jax.numpy as jnp
import numpy as np
from jax import lax
from jax.experimental import pallas as pl
from jax.experimental.pallas import tpu as pltpu
from jax.sharding import PartitionSpec as P

OMEGA = 0.15
NV = 5
NH = 11
NT = 24
OWN = 12
ROWS = 16
VR = NV * ROWS
FR = 64
MESH = pl.DeviceIdType.MESH
F32 = jnp.float32
BF16 = jnp.bfloat16


def constants():
    t = np.arange(NT)
    d = t[:, None] - t[None, :]
    skewed = np.zeros((NT, NT))
    for k in range(1, NH + 1):
        skewed -= 2.0 / NT * k * np.sin(2 * np.pi * ((k * d) % NT) / NT)
    derivative = 0.5 * skewed - 0.5 * skewed.T
    big = np.zeros((NV, ROWS, 2, NV, ROWS))
    for j in range(NV):
        for h in range(2):
            big[j, :OWN, h, j, :OWN] = OMEGA * derivative[:OWN, h * OWN : (h + 1) * OWN]
    big = big.reshape(VR, 2 * VR).astype(np.float32)
    hi = big.astype(BF16)
    lo = (big - hi.astype(np.float32)).astype(BF16)
    deriv = np.concatenate([hi, lo], 0)
    a1 = np.zeros((FR, 128))
    a2 = np.zeros((FR, 128))
    f = np.zeros((128, 2, NV, ROWS))
    order = np.full((1, 128), -1, np.int32)
    tt = np.arange(OWN)
    for j in range(NV):
        rows = j * OWN + tt
        for m in range(NT):
            lane = j * NT + m
            k = (m + 1) // 2
            for h in range(2):
                s = tt + h * OWN
                if m == 0:
                    f[lane, h, j, :OWN] = 1.0 / NT
                elif m == NT - 1:
                    f[lane, h, j, :OWN] = (1.0 - 2.0 * (s % 2)) / NT
                elif m % 2 == 1:
                    f[lane, h, j, :OWN] = 2.0 / NT * np.cos(2 * np.pi * ((k * s) % NT) / NT)
                else:
                    f[lane, h, j, :OWN] = 2.0 / NT * np.sin(2 * np.pi * ((k * s) % NT) / NT)
            arc = 2 * np.pi * ((k * tt) % NT) / NT
            if m == 0:
                a1[rows, lane] = 1.0
            elif m == NT - 1:
                a1[rows, lane] = 1.0 - 2.0 * (tt % 2)
            elif m % 2 == 1:
                a1[rows, lane], a2[rows, lane] = np.cos(arc), np.sin(arc)
                order[0, lane] = k - 1
            else:
                a1[rows, lane], a2[rows, lane] = np.sin(arc), -np.cos(arc)
                order[0, lane] = k - 1
    f = f.reshape(128, 2 * VR)
    perm = np.zeros((NV * NV, ROWS, OWN, 32), np.float32)
    for e in range(NV * NV):
        for i in range(OWN):
            perm[e, i, i, e] = 1.0
    perm = perm.reshape(NV * NV * ROWS, OWN * 32).astype(BF16)
    return (
        deriv,
        np.concatenate([a1, a2], 0).astype(np.float32),
        f.astype(np.float32),
        order,
        perm,
    )


def split(x):
    hi = x.astype(BF16)
    return hi, (x - hi.astype(F32)).astype(BF16)


def dot(a, b):
    return jnp.dot(a, b, preferred_element_type=F32)


def dot_t(a, b):
    return lax.dot_general(a, b, (((1,), (1,)), ((), ())), preferred_element_type=F32)


def kernel(
    passages,
    tan_hbm, adj_hbm, jac_hbm, pre_hbm, upwind_ref, upw_ref, bot_ref, up_ref, lo_ref, phase_ref,
    deriv_ref, a_ref, f_ref, order_ref, perm_ref,
    tan_out, adj_out,
    tan_own, adj_own, tan_far, jac, pre, mpad, jt, pt,
    vt, vd, vfar, dual_far, sel_lo, sel_up, send, recv, spread, img, stage, adj_stage,
    in_sem, out_sem, send_sem, recv_sem,
):
    blade, inst = lax.axis_index("blade"), lax.axis_index("inst")
    ring = lax.axis_size("blade")
    nxt = {"blade": lax.rem(blade + 1, ring)}
    prv = {"blade": lax.rem(blade + ring - 1, ring)}
    sib = {"inst": 1 - inst}

    loads = [
        pltpu.make_async_copy(src.at[0], dst, in_sem.at[n])
        for n, (src, dst) in enumerate(
            ((adj_hbm, adj_own), (pre_hbm, pre), (tan_hbm, tan_own), (jac_hbm, jac))
        )
    ]
    for copy in loads:
        copy.start()

    barrier = pltpu.get_barrier_semaphore()
    for device in (sib, prv, nxt):
        pl.semaphore_signal(barrier, inc=1, device_id=device, device_id_type=MESH)

    def remote(n, src, dst, device):
        return pltpu.make_async_remote_copy(
            src_ref=src, dst_ref=dst, send_sem=send_sem.at[n], recv_sem=recv_sem.at[n],
            device_id=device, device_id_type=MESH,
        )

    send_tan = remote(0, tan_hbm.at[0], tan_far, sib)
    send_dual = remote(1, vd, dual_far, sib)
    face_sends = [
        remote(2, send.at[0], recv.at[0], prv),
        remote(3, send.at[1], recv.at[1], nxt),
        remote(4, send.at[2], recv.at[2], prv),
        remote(5, send.at[3], recv.at[3], nxt),
    ]

    pl.semaphore_wait(barrier, 3)
    send_tan.start()

    order = order_ref[...]
    index = jnp.zeros((1, 128), F32)
    for k in range(NH):
        index = jnp.where(order == k, phase_ref[k].astype(F32), index)
    angle = (2.0 * math.pi / passages) * index
    cosine, sine = jnp.cos(angle), jnp.sin(angle)
    a1, a2 = a_ref[:FR], a_ref[FR:]
    both = jnp.concatenate([a1 * cosine + a2 * sine, a1 * cosine - a2 * sine], 0)
    rot = jnp.dot(both, f_ref[...], preferred_element_type=F32, precision=lax.Precision.HIGHEST)
    rot_lo, rot_up = [jnp.concatenate(split(rot[n * FR : (n + 1) * FR]), 0) for n in range(2)]

    for table, sel in ((lo_ref, sel_lo), (up_ref, sel_up)):
        for h in range(2):
            cells = lax.broadcasted_iota(jnp.int32, (512, 128), 0) + 512 * h
            hit = cells == table[:, 128 * h : 128 * h + 128]
            sel[h] = jnp.where(hit, 1.0, 0.0).astype(BF16)

    vt[...] = jnp.zeros_like(vt)
    vfar[...] = jnp.zeros_like(vfar)
    mpad[...] = jnp.zeros_like(mpad)
    spread[...] = jnp.zeros_like(spread)

    def regroup(src, dst):
        for t in range(OWN):
            mpad[t, 0:25, :] = src[t]
        for n in range(4):
            lanes = slice(256 * n, 256 * n + 256)
            part = mpad[:, :, lanes].reshape(OWN * 32, 256)
            dst[:, :, lanes] = dot(perm_ref[...], part).reshape(NV * NV, ROWS, 256)

    def block(m, src, i, lanes, transposed):
        total = None
        for j in range(NV):
            e = j * NV + i if transposed else i * NV + j
            term = m[e, :, lanes] * src[j, :, lanes]
            total = term if total is None else total + term
        return total

    loads[0].wait()
    loads[1].wait()
    for j in range(NV):
        vfar[j, 0:OWN, :] = adj_own[j]
    regroup(pre, pt)
    for n in range(8):
        lanes = slice(128 * n, 128 * n + 128)
        for i in range(NV):
            vd[i, :, lanes] = block(pt, vfar, i, lanes, True)
    send_dual.start()

    def faces(field_hi, field_lo, base):
        halves = jnp.concatenate([field_hi, field_lo], 0)
        for n, (sel, rotation) in enumerate(((sel_lo, rot_lo), (sel_up, rot_up))):
            picked = jnp.concatenate(
                [dot(halves[:, 512 * h : 512 * h + 512], sel[h]) for h in range(2)], 1
            ).astype(BF16)
            turned = dot(rotation, picked[: 2 * VR])
            total = turned[:FR] + turned[FR:] + dot(rotation[:FR], picked[2 * VR :])
            if base == 2:
                total = total * (bot_ref[...] if n == 0 else upw_ref[...])
            send[base + n] = total
            face_sends[base + n].start()

    def mixed(field_hi, field_lo):
        twice = dot(deriv_ref[...], field_hi)
        return twice[:VR] + twice[VR:] + dot(deriv_ref[:VR], field_lo)

    def field(own, far):
        return split(jnp.concatenate([own.reshape(VR, 1024), far.reshape(VR, 1024)], 0))

    loads[2].wait()
    for j in range(NV):
        vt[j, 0:OWN, :] = tan_own[j]
    send_tan.wait()
    for j in range(NV):
        vfar[j, 0:OWN, :] = tan_far[j]
    tan_hi, tan_lo = field(vt[...], vfar[...])
    faces(tan_hi, tan_lo, 0)
    img[0] = mixed(tan_hi, tan_lo).reshape(NV, ROWS, 1024)

    send_dual.wait()
    dual_hi, dual_lo = field(vd[...], dual_far[...])
    faces(dual_hi, dual_lo, 2)
    img[1] = -mixed(dual_hi, dual_lo).reshape(NV, ROWS, 1024)

    loads[3].wait()
    regroup(jac, jt)
    lane = lax.broadcasted_iota(jnp.int32, (ROWS, 1024), 1)
    upwind = upwind_ref[...]
    for i in range(NV):
        before = jnp.where(lane == 0, 0.0, pltpu.roll(vt[i], 1, 1))
        img[0, i] = img[0, i] - upwind * before
        after = jnp.where(lane == 1023, 0.0, pltpu.roll(upwind * vd[i], 1023, 1))
        img[1, i] = img[1, i] - after
    for n in range(8):
        lanes = slice(128 * n, 128 * n + 128)
        for i in range(NV):
            img[0, i, :, lanes] = img[0, i, :, lanes] + block(jt, vt, i, lanes, False)
            img[1, i, :, lanes] = img[1, i, :, lanes] + block(jt, vd, i, lanes, True)

    def add_faces(base, scales):
        for n in range(2):
            for j in range(NV):
                got = recv[base + n, j * OWN : j * OWN + OWN, :]
                spread[n, j, 0:OWN, :] = got if scales is None else got * scales[n][...]
        pair = [jnp.concatenate(split(spread[n].reshape(VR, 256)), 0) for n in range(2)]
        for h in range(2):
            cells = slice(512 * h, 512 * h + 512)
            part = slice(128 * h, 128 * h + 128)
            total = dot_t(pair[0][:, part], sel_up[h]) + dot_t(pair[1][:, part], sel_lo[h])
            total = (total[:VR] + total[VR:]).reshape(NV, ROWS, 512)
            img[base // 2, :, :, cells] = img[base // 2, :, :, cells] - total

    for copy in face_sends[:2]:
        copy.wait()
    add_faces(0, (upw_ref, bot_ref))
    for n in range(8):
        lanes = slice(128 * n, 128 * n + 128)
        for i in range(NV):
            stage[i, :, lanes] = block(pt, img.at[0], i, lanes, False)[:OWN]
    tan_store = pltpu.make_async_copy(stage, tan_out.at[0], out_sem.at[0])
    tan_store.start()

    for copy in face_sends[2:]:
        copy.wait()
    add_faces(2, None)
    adj_stage[...] = img[1, :, 0:OWN, :]
    adj_store = pltpu.make_async_copy(adj_stage, adj_out.at[0], out_sem.at[1])
    adj_store.start()
    tan_store.wait()
    adj_store.wait()


def on_device(
    tangent_seed, adjoint_seed, jacobian, precond, upwind, up_weight, bottom_face_strength,
    up_cells, lo_cells, phase_index,
):
    passages = tangent_seed.shape[0] * lax.axis_size("blade")
    deriv, a, f, order, perm = constants()
    field = (NV, ROWS, 1024)
    whole = pl.BlockSpec(memory_space=pltpu.VMEM)
    hbm = pl.BlockSpec(memory_space=pl.ANY)
    return pl.pallas_call(
        functools.partial(kernel, passages),
        out_shape=(
            jax.ShapeDtypeStruct(tangent_seed.shape, F32),
            jax.ShapeDtypeStruct(adjoint_seed.shape, F32),
        ),
        in_specs=[hbm] * 4 + [whole] * 5 + [pl.BlockSpec(memory_space=pltpu.SMEM)] + [whole] * 5,
        out_specs=(hbm, hbm),
        scratch_shapes=[
            pltpu.VMEM((NV, OWN, 1024), F32),
            pltpu.VMEM((NV, OWN, 1024), F32),
            pltpu.VMEM((NV, OWN, 1024), F32),
            pltpu.VMEM((OWN, 25, 1024), BF16),
            pltpu.VMEM((OWN, 25, 1024), BF16),
            pltpu.VMEM((OWN, 32, 1024), BF16),
            pltpu.VMEM((25, ROWS, 1024), F32),
            pltpu.VMEM((25, ROWS, 1024), F32),
            pltpu.VMEM(field, F32),
            pltpu.VMEM(field, F32),
            pltpu.VMEM(field, F32),
            pltpu.VMEM(field, F32),
            pltpu.VMEM((2, 512, 128), BF16),
            pltpu.VMEM((2, 512, 128), BF16),
            pltpu.VMEM((4, FR, 256), F32),
            pltpu.VMEM((4, FR, 256), F32),
            pltpu.VMEM((2, NV, ROWS, 256), F32),
            pltpu.VMEM((2,) + field, F32),
            pltpu.VMEM((NV, OWN, 1024), F32),
            pltpu.VMEM((NV, OWN, 1024), F32),
            pltpu.SemaphoreType.DMA((4,)),
            pltpu.SemaphoreType.DMA((2,)),
            pltpu.SemaphoreType.DMA((6,)),
            pltpu.SemaphoreType.DMA((6,)),
        ],
        compiler_params=pltpu.CompilerParams(
            collective_id=0, has_side_effects=True, vmem_limit_bytes=48 * 1024 * 1024
        ),
        name="harmonic_blade_row",
    )(
        tangent_seed, adjoint_seed, jacobian, precond, upwind, up_weight, bottom_face_strength,
        up_cells.reshape(1, -1), lo_cells.reshape(1, -1), phase_index,
        deriv, a, f, order, perm,
    )


def solution(mesh):
    in_specs = (
        P("blade", None, "inst", None),
        P("blade", None, "inst", None),
        P("blade", "inst", None, None),
        P("blade", "inst", None, None),
        P("blade", None),
        P("blade", None),
        P("blade", None),
        P(),
        P(),
        P(),
    )
    out_specs = (P("blade", None, "inst", None), P("blade", None, "inst", None))
    return jax.shard_map(
        on_device, mesh=mesh, in_specs=in_specs, out_specs=out_specs, check_vma=False
    )
```

```python
import functools
import math

import jax
import jax.numpy as jnp
import numpy as np
from jax import lax
from jax.experimental import pallas as pl
from jax.experimental.pallas import tpu as pltpu
from jax.sharding import PartitionSpec as P

OMEGA = 0.15
NV = 5
NH = 11
NT = 24
OWN = 12
ROWS = 16
VR = NV * ROWS
FR = 64
VMEM_LIMIT = 63 * 1024 * 1024
MESH = pl.DeviceIdType.MESH
F32 = jnp.float32
BF16 = jnp.bfloat16


def constants():
    t = np.arange(NT)
    d = t[:, None] - t[None, :]
    skewed = np.zeros((NT, NT))
    for k in range(1, NH + 1):
        skewed -= 2.0 / NT * k * np.sin(2 * np.pi * ((k * d) % NT) / NT)
    derivative = 0.5 * skewed - 0.5 * skewed.T
    big = np.zeros((NV, ROWS, 2, NV, ROWS))
    for j in range(NV):
        for h in range(2):
            big[j, :OWN, h, j, :OWN] = OMEGA * derivative[:OWN, h * OWN : (h + 1) * OWN]
    big = big.reshape(VR, 2 * VR).astype(np.float32)
    hi = big.astype(BF16)
    lo = (big - hi.astype(np.float32)).astype(BF16)
    deriv = np.concatenate([hi, lo], 0)
    a1 = np.zeros((FR, 128))
    a2 = np.zeros((FR, 128))
    f = np.zeros((128, 2, NV, ROWS))
    order = np.full((1, 128), -1, np.int32)
    tt = np.arange(OWN)
    for j in range(NV):
        rows = j * OWN + tt
        for m in range(NT):
            lane = j * NT + m
            k = (m + 1) // 2
            for h in range(2):
                s = tt + h * OWN
                if m == 0:
                    f[lane, h, j, :OWN] = 1.0 / NT
                elif m == NT - 1:
                    f[lane, h, j, :OWN] = (1.0 - 2.0 * (s % 2)) / NT
                elif m % 2 == 1:
                    f[lane, h, j, :OWN] = 2.0 / NT * np.cos(2 * np.pi * ((k * s) % NT) / NT)
                else:
                    f[lane, h, j, :OWN] = 2.0 / NT * np.sin(2 * np.pi * ((k * s) % NT) / NT)
            arc = 2 * np.pi * ((k * tt) % NT) / NT
            if m == 0:
                a1[rows, lane] = 1.0
            elif m == NT - 1:
                a1[rows, lane] = 1.0 - 2.0 * (tt % 2)
            elif m % 2 == 1:
                a1[rows, lane], a2[rows, lane] = np.cos(arc), np.sin(arc)
                order[0, lane] = k - 1
            else:
                a1[rows, lane], a2[rows, lane] = np.sin(arc), -np.cos(arc)
                order[0, lane] = k - 1
    f = f.reshape(128, 2 * VR)
    return (
        deriv,
        np.concatenate([a1, a2], 0).astype(np.float32),
        f.astype(np.float32),
        order,
    )


def split(x):
    hi = x.astype(BF16)
    return hi, (x - hi.astype(F32)).astype(BF16)


def dot(a, b):
    return jnp.dot(a, b, preferred_element_type=F32)


def dot_t(a, b):
    return lax.dot_general(a, b, (((1,), (1,)), ((), ())), preferred_element_type=F32)


def kernel(
    passages,
    tan_hbm, adj_hbm, jac_hbm, pre_hbm, upwind_hbm, upw_hbm, bot_hbm, up_hbm, lo_hbm, phase_hbm,
    deriv_hbm, a_hbm, f_hbm, order_hbm,
    tan_out, adj_out,
    upwind_ref, upw_ref, bot_ref, up_ref, lo_ref, phase_ref, deriv_ref, a_ref, f_ref, order_ref,
    tan_own, adj_own, tan_far, jac, pre, mpad, perm, jt, pt,
    vt, vd, va, vfar, dual_far, sel_lo, sel_up, send, recv, spread, img, tan_stage, adj_stage,
    in_sem, tan_sem, adj_sem, tan_out_sem, adj_out_sem, far_send, far_recv, send_sem, recv_sem,
):
    blade, inst = lax.axis_index("blade"), lax.axis_index("inst")
    ring = lax.axis_size("blade")
    nxt = {"blade": lax.rem(blade + 1, ring)}
    prv = {"blade": lax.rem(blade + ring - 1, ring)}
    sib = {"inst": 1 - inst}

    barrier = pltpu.get_barrier_semaphore()
    for device in (sib, prv, nxt):
        pl.semaphore_signal(barrier, inc=1, device_id=device, device_id_type=MESH)

    def chunk(n):
        return slice(128 * n, 128 * n + 128)

    def load(n, src, dst):
        return pltpu.make_async_copy(src, dst, in_sem.at[n])

    def seed_loads(src, dst, sems):
        return [
            pltpu.make_async_copy(src.at[:, :, n, 0, :], dst.at[:, :, chunk(n)], sems.at[n])
            for n in range(8)
        ]

    first = [
        load(n, src, dst)
        for n, (src, dst) in enumerate(
            (
                (phase_hbm, phase_ref), (order_hbm, order_ref), (a_hbm, a_ref), (f_hbm, f_ref),
                (lo_hbm, lo_ref), (up_hbm, up_ref),
            )
        )
    ]
    tan_loads = seed_loads(tan_hbm, tan_own, tan_sem)
    adj_loads = seed_loads(adj_hbm, adj_own, adj_sem)
    pre_load = load(6, pre_hbm.at[0], pre)
    weights = [load(7, upw_hbm, upw_ref), load(8, bot_hbm, bot_ref), load(9, upwind_hbm, upwind_ref)]
    deriv_load = load(10, deriv_hbm, deriv_ref)
    jac_load = load(11, jac_hbm.at[0], jac)
    for copy in first + tan_loads + [pre_load] + adj_loads + weights + [deriv_load, jac_load]:
        copy.start()

    def remote(n, src, dst, device):
        return pltpu.make_async_remote_copy(
            src_ref=src, dst_ref=dst, send_sem=send_sem.at[n], recv_sem=recv_sem.at[n],
            device_id=device, device_id_type=MESH,
        )

    tan_sends = [
        pltpu.make_async_remote_copy(
            src_ref=tan_hbm.at[:, :, n, 0, :], dst_ref=tan_far.at[:, :, chunk(n)],
            send_sem=far_send.at[n], recv_sem=far_recv.at[n],
            device_id=sib, device_id_type=MESH,
        )
        for n in range(8)
    ]
    send_dual = remote(0, vd, dual_far, sib)
    face_sends = [
        remote(1, send.at[0], recv.at[0], prv),
        remote(2, send.at[1], recv.at[1], nxt),
        remote(3, send.at[2], recv.at[2], prv),
        remote(4, send.at[3], recv.at[3], nxt),
    ]

    row = lax.broadcasted_iota(jnp.int32, (NV * NV * ROWS, 1), 0)
    source = (row & (ROWS - 1)) * 32 + (row >> 4)
    column = lax.broadcasted_iota(jnp.int32, (NV * NV * ROWS, OWN * 32), 1)
    perm[...] = jnp.where(column == source, 1.0, 0.0).astype(BF16)
    vt[:, 8:, :] = jnp.zeros((NV, 8, 1024), F32)
    va[:, 8:, :] = jnp.zeros((NV, 8, 1024), F32)
    vfar[:, 8:, :] = jnp.zeros((NV, 8, 1024), F32)
    mpad[:, 16:, :] = jnp.zeros((OWN, 16, 1024), BF16)
    spread[:, :, 8:, :] = jnp.zeros((2, NV, 8, 256), F32)

    pl.semaphore_wait(barrier, 3)
    for copy in tan_sends:
        copy.start()

    for copy in first:
        copy.wait()
    order = order_ref[...]
    index = jnp.zeros((1, 128), F32)
    for k in range(NH):
        index = jnp.where(order == k, phase_ref[k].astype(F32), index)
    angle = (2.0 * math.pi / passages) * index
    cosine, sine = jnp.cos(angle), jnp.sin(angle)
    a1, a2 = a_ref[:FR], a_ref[FR:]
    both = jnp.concatenate([a1 * cosine + a2 * sine, a1 * cosine - a2 * sine], 0)
    rot = jnp.dot(both, f_ref[...], preferred_element_type=F32, precision=lax.Precision.HIGHEST)
    rot_lo, rot_up = [jnp.concatenate(split(rot[n * FR : (n + 1) * FR]), 0) for n in range(2)]

    for table, sel in ((lo_ref, sel_lo), (up_ref, sel_up)):
        for h in range(2):
            cells = lax.broadcasted_iota(jnp.int32, (512, 128), 0) + 512 * h
            hit = cells == table[:, 128 * h : 128 * h + 128]
            sel[h] = jnp.where(hit, 1.0, 0.0).astype(BF16)

    def regroup(src, dst):
        for t in range(OWN):
            mpad[t, 0:25, :] = src[t]
        for n in range(4):
            lanes = slice(256 * n, 256 * n + 256)
            part = mpad[:, :, lanes].reshape(OWN * 32, 256)
            dst[:, :, lanes] = dot(perm[...], part).reshape(NV * NV, ROWS, 256)

    def block(m, src, i, lanes, transposed):
        total = None
        for j in range(NV):
            e = j * NV + i if transposed else i * NV + j
            term = m[e, :, lanes] * src[j, :, lanes]
            total = term if total is None else total + term
        return total

    def faces(field_hi, field_lo, base):
        halves = jnp.concatenate([field_hi, field_lo], 0)
        for n, (sel, rotation) in enumerate(((sel_lo, rot_lo), (sel_up, rot_up))):
            picked = jnp.concatenate(
                [dot(halves[:, 512 * h : 512 * h + 512], sel[h]) for h in range(2)], 1
            ).astype(BF16)
            turned = dot(rotation, picked[: 2 * VR])
            total = turned[:FR] + turned[FR:] + dot(rotation[:FR], picked[2 * VR :])
            if base == 2:
                total = total * (bot_ref[...] if n == 0 else upw_ref[...])
            send[base + n] = total
            face_sends[base + n].start()

    def mixed(field_hi, field_lo):
        twice = dot(deriv_ref[...], field_hi)
        return twice[:VR] + twice[VR:] + dot(deriv_ref[:VR], field_lo)

    def field(own, far):
        return split(jnp.concatenate([own.reshape(VR, 1024), far.reshape(VR, 1024)], 0))

    for copy in tan_loads:
        copy.wait()
    for j in range(NV):
        vt[j, 0:OWN, :] = tan_own[j]
    for copy in tan_sends:
        copy.wait()
    for j in range(NV):
        vfar[j, 0:OWN, :] = tan_far[j]
    tan_hi, tan_lo = field(vt[...], vfar[...])
    faces(tan_hi, tan_lo, 0)

    pre_load.wait()
    regroup(pre, pt)
    for copy in adj_loads:
        copy.wait()
    for j in range(NV):
        va[j, 0:OWN, :] = adj_own[j]
    for n in range(8):
        for i in range(NV):
            vd[i, :, chunk(n)] = block(pt, va, i, chunk(n), True)
    send_dual.start()

    for copy in weights:
        copy.wait()
    deriv_load.wait()
    img[0] = mixed(tan_hi, tan_lo).reshape(NV, ROWS, 1024)
    jac_load.wait()
    regroup(jac, jt)
    lane = lax.broadcasted_iota(jnp.int32, (ROWS, 1024), 1)
    upwind = upwind_ref[...]

    send_dual.wait()
    dual_hi, dual_lo = field(vd[...], dual_far[...])
    faces(dual_hi, dual_lo, 2)

    for i in range(NV):
        before = jnp.where(lane == 0, 0.0, pltpu.roll(vt[i], 1, 1))
        img[0, i] = img[0, i] - upwind * before
    for n in range(8):
        for i in range(NV):
            img[0, i, :, chunk(n)] = img[0, i, :, chunk(n)] + block(jt, vt, i, chunk(n), False)

    img[1] = -mixed(dual_hi, dual_lo).reshape(NV, ROWS, 1024)
    for i in range(NV):
        after = jnp.where(lane == 1023, 0.0, pltpu.roll(upwind * vd[i], 1023, 1))
        img[1, i] = img[1, i] - after
    for n in range(8):
        for i in range(NV):
            img[1, i, :, chunk(n)] = img[1, i, :, chunk(n)] + block(jt, vd, i, chunk(n), True)

    def add_faces(base, scales):
        for n in range(2):
            for j in range(NV):
                got = recv[base + n, j * OWN : j * OWN + OWN, :]
                spread[n, j, 0:OWN, :] = got if scales is None else got * scales[n][...]
        pair = [jnp.concatenate(split(spread[n].reshape(VR, 256)), 0) for n in range(2)]
        for h in range(2):
            cells = slice(512 * h, 512 * h + 512)
            part = slice(128 * h, 128 * h + 128)
            total = dot_t(pair[0][:, part], sel_up[h]) + dot_t(pair[1][:, part], sel_lo[h])
            total = (total[:VR] + total[VR:]).reshape(NV, ROWS, 512)
            img[base // 2, :, :, cells] = img[base // 2, :, :, cells] - total

    def stores(src, dst, sems):
        return [
            pltpu.make_async_copy(src.at[:, :, chunk(n)], dst.at[:, :, n, 0, :], sems.at[n])
            for n in range(8)
        ]

    tan_stores = stores(tan_stage, tan_out, tan_out_sem)
    adj_stores = stores(adj_stage, adj_out, adj_out_sem)

    for copy in face_sends[:2]:
        copy.wait()
    add_faces(0, (upw_ref, bot_ref))
    for n in range(8):
        for i in range(NV):
            tan_stage[i, :, chunk(n)] = block(pt, img.at[0], i, chunk(n), False)[:OWN]
        tan_stores[n].start()

    for copy in face_sends[2:]:
        copy.wait()
    add_faces(2, None)
    for n in range(8):
        adj_stage[:, :, chunk(n)] = img[1, :, 0:OWN, chunk(n)]
        adj_stores[n].start()
    for copy in tan_stores + adj_stores:
        copy.wait()


def on_device(
    tangent_seed, adjoint_seed, jacobian, precond, upwind, up_weight, bottom_face_strength,
    up_cells, lo_cells, phase_index,
):
    passages = tangent_seed.shape[0] * lax.axis_size("blade")
    deriv, a, f, order = constants()
    own = (NV, OWN, 1024)
    field = (NV, ROWS, 1024)
    linear = (NV, OWN, 8, 1, 128)
    hbm = pl.BlockSpec(memory_space=pl.ANY)
    tangent_out, adjoint_out = pl.pallas_call(
        functools.partial(kernel, passages),
        out_shape=(jax.ShapeDtypeStruct(linear, F32), jax.ShapeDtypeStruct(linear, F32)),
        in_specs=[hbm] * 14,
        out_specs=(hbm, hbm),
        scratch_shapes=[
            pltpu.VMEM((1, 1024), F32),
            pltpu.VMEM((1, 256), F32),
            pltpu.VMEM((1, 256), F32),
            pltpu.VMEM((1, 256), jnp.int32),
            pltpu.VMEM((1, 256), jnp.int32),
            pltpu.SMEM((NH,), jnp.int32),
            pltpu.VMEM(deriv.shape, BF16),
            pltpu.VMEM(a.shape, F32),
            pltpu.VMEM(f.shape, F32),
            pltpu.VMEM(order.shape, jnp.int32),
            pltpu.VMEM(own, F32),
            pltpu.VMEM(own, F32),
            pltpu.VMEM(own, F32),
            pltpu.VMEM((OWN, 25, 1024), BF16),
            pltpu.VMEM((OWN, 25, 1024), BF16),
            pltpu.VMEM((OWN, 32, 1024), BF16),
            pltpu.VMEM((NV * NV * ROWS, OWN * 32), BF16),
            pltpu.VMEM((25, ROWS, 1024), F32),
            pltpu.VMEM((25, ROWS, 1024), F32),
            pltpu.VMEM(field, F32),
            pltpu.VMEM(field, F32),
            pltpu.VMEM(field, F32),
            pltpu.VMEM(field, F32),
            pltpu.VMEM(field, F32),
            pltpu.VMEM((2, 512, 128), BF16),
            pltpu.VMEM((2, 512, 128), BF16),
            pltpu.VMEM((4, FR, 256), F32),
            pltpu.VMEM((4, FR, 256), F32),
            pltpu.VMEM((2, NV, ROWS, 256), F32),
            pltpu.VMEM((2,) + field, F32),
            pltpu.VMEM(own, F32),
            pltpu.VMEM(own, F32),
            pltpu.SemaphoreType.DMA((12,)),
            pltpu.SemaphoreType.DMA((8,)),
            pltpu.SemaphoreType.DMA((8,)),
            pltpu.SemaphoreType.DMA((8,)),
            pltpu.SemaphoreType.DMA((8,)),
            pltpu.SemaphoreType.DMA((8,)),
            pltpu.SemaphoreType.DMA((8,)),
            pltpu.SemaphoreType.DMA((5,)),
            pltpu.SemaphoreType.DMA((5,)),
        ],
        compiler_params=pltpu.CompilerParams(
            collective_id=0, has_side_effects=True, vmem_limit_bytes=VMEM_LIMIT
        ),
        name="harmonic_blade_row",
    )(
        tangent_seed.reshape(linear), adjoint_seed.reshape(linear), jacobian, precond,
        upwind, up_weight, bottom_face_strength,
        up_cells.reshape(1, -1), lo_cells.reshape(1, -1), phase_index,
        deriv, a, f, order,
    )
    return (tangent_out.reshape(tangent_seed.shape), adjoint_out.reshape(adjoint_seed.shape))


def solution(mesh):
    in_specs = (
        P("blade", None, "inst", None),
        P("blade", None, "inst", None),
        P("blade", "inst", None, None),
        P("blade", "inst", None, None),
        P("blade", None),
        P("blade", None),
        P("blade", None),
        P(),
        P(),
        P(),
    )
    out_specs = (P("blade", None, "inst", None), P("blade", None, "inst", None))
    return jax.shard_map(
        on_device, mesh=mesh, in_specs=in_specs, out_specs=out_specs, check_vma=False
    )
```

```python
import functools
import math

import jax
import jax.numpy as jnp
import numpy as np
from jax import lax
from jax.experimental import pallas as pl
from jax.experimental.pallas import tpu as pltpu
from jax.sharding import PartitionSpec as P

OMEGA = 0.15
NV = 5
NH = 11
NT = 24
OWN = 12
ROWS = 16
VR = NV * ROWS
FR = 64
VMEM_LIMIT = 63 * 1024 * 1024
MESH = pl.DeviceIdType.MESH
F32 = jnp.float32
BF16 = jnp.bfloat16


def constants():
    t = np.arange(NT)
    d = t[:, None] - t[None, :]
    skewed = np.zeros((NT, NT))
    for k in range(1, NH + 1):
        skewed -= 2.0 / NT * k * np.sin(2 * np.pi * ((k * d) % NT) / NT)
    derivative = 0.5 * skewed - 0.5 * skewed.T
    big = np.zeros((NV, ROWS, 2, NV, ROWS))
    for j in range(NV):
        for h in range(2):
            big[j, :OWN, h, j, :OWN] = OMEGA * derivative[:OWN, h * OWN : (h + 1) * OWN]
    big = big.reshape(VR, 2 * VR).astype(np.float32)
    hi = big.astype(BF16)
    lo = (big - hi.astype(np.float32)).astype(BF16)
    deriv = np.concatenate([hi, lo], 0)
    a1 = np.zeros((FR, 128))
    a2 = np.zeros((FR, 128))
    f = np.zeros((128, 2, NV, ROWS))
    order = np.full((1, 128), -1, np.int32)
    tt = np.arange(OWN)
    for j in range(NV):
        rows = j * OWN + tt
        for m in range(NT):
            lane = j * NT + m
            k = (m + 1) // 2
            for h in range(2):
                s = tt + h * OWN
                if m == 0:
                    f[lane, h, j, :OWN] = 1.0 / NT
                elif m == NT - 1:
                    f[lane, h, j, :OWN] = (1.0 - 2.0 * (s % 2)) / NT
                elif m % 2 == 1:
                    f[lane, h, j, :OWN] = 2.0 / NT * np.cos(2 * np.pi * ((k * s) % NT) / NT)
                else:
                    f[lane, h, j, :OWN] = 2.0 / NT * np.sin(2 * np.pi * ((k * s) % NT) / NT)
            arc = 2 * np.pi * ((k * tt) % NT) / NT
            if m == 0:
                a1[rows, lane] = 1.0
            elif m == NT - 1:
                a1[rows, lane] = 1.0 - 2.0 * (tt % 2)
            elif m % 2 == 1:
                a1[rows, lane], a2[rows, lane] = np.cos(arc), np.sin(arc)
                order[0, lane] = k - 1
            else:
                a1[rows, lane], a2[rows, lane] = np.sin(arc), -np.cos(arc)
                order[0, lane] = k - 1
    f = f.reshape(128, 2 * VR)
    return (
        deriv,
        np.concatenate([a1, a2], 0).astype(np.float32),
        f.astype(np.float32),
        order,
    )


def split(x):
    hi = x.astype(BF16)
    return hi, (x - hi.astype(F32)).astype(BF16)


def dot(a, b):
    return jnp.dot(a, b, preferred_element_type=F32)


def dot_t(a, b):
    return lax.dot_general(a, b, (((1,), (1,)), ((), ())), preferred_element_type=F32)


def kernel(
    passages,
    tan_hbm, adj_hbm, jac_hbm, pre_hbm, upwind_hbm, upw_hbm, bot_hbm, up_hbm, lo_hbm, phase_hbm,
    deriv_hbm, a_hbm, f_hbm, order_hbm,
    tan_stage, adj_stage,
    upwind_ref, upw_ref, bot_ref, up_ref, lo_ref, phase_ref, deriv_ref, a_ref, f_ref, order_ref,
    tan_own, adj_own, tan_far, jac, pre, mpad, perm, jt, pt,
    vt, vd, va, vfar, dual_far, sel_lo, sel_up, send, recv, spread, img,
    in_sem, tan_sem, adj_sem, far_send, far_recv, send_sem, recv_sem,
):
    blade, inst = lax.axis_index("blade"), lax.axis_index("inst")
    ring = lax.axis_size("blade")
    nxt = {"blade": lax.rem(blade + 1, ring)}
    prv = {"blade": lax.rem(blade + ring - 1, ring)}
    sib = {"inst": 1 - inst}

    barrier = pltpu.get_barrier_semaphore()
    for device in (sib, prv, nxt):
        pl.semaphore_signal(barrier, inc=1, device_id=device, device_id_type=MESH)

    def chunk(n):
        return slice(128 * n, 128 * n + 128)

    def load(n, src, dst):
        return pltpu.make_async_copy(src, dst, in_sem.at[n])

    def seed_loads(src, dst, sems):
        return [
            pltpu.make_async_copy(src.at[:, :, n, 0, :], dst.at[:, :, chunk(n)], sems.at[n])
            for n in range(8)
        ]

    first = [
        load(n, src, dst)
        for n, (src, dst) in enumerate(
            (
                (phase_hbm, phase_ref), (order_hbm, order_ref), (a_hbm, a_ref), (f_hbm, f_ref),
                (lo_hbm, lo_ref), (up_hbm, up_ref),
            )
        )
    ]
    tan_loads = seed_loads(tan_hbm, tan_own, tan_sem)
    adj_loads = seed_loads(adj_hbm, adj_own, adj_sem)
    pre_load = load(6, pre_hbm.at[0], pre)
    weights = [load(7, upw_hbm, upw_ref), load(8, bot_hbm, bot_ref), load(9, upwind_hbm, upwind_ref)]
    deriv_load = load(10, deriv_hbm, deriv_ref)
    jac_load = load(11, jac_hbm.at[0], jac)
    for copy in first + tan_loads + [pre_load] + adj_loads + weights + [deriv_load, jac_load]:
        copy.start()

    def remote(n, src, dst, device):
        return pltpu.make_async_remote_copy(
            src_ref=src, dst_ref=dst, send_sem=send_sem.at[n], recv_sem=recv_sem.at[n],
            device_id=device, device_id_type=MESH,
        )

    tan_sends = [
        pltpu.make_async_remote_copy(
            src_ref=tan_hbm.at[:, :, n, 0, :], dst_ref=tan_far.at[:, :, chunk(n)],
            send_sem=far_send.at[n], recv_sem=far_recv.at[n],
            device_id=sib, device_id_type=MESH,
        )
        for n in range(8)
    ]
    send_dual = remote(0, vd, dual_far, sib)
    face_sends = [
        remote(1, send.at[0], recv.at[0], prv),
        remote(2, send.at[1], recv.at[1], nxt),
        remote(3, send.at[2], recv.at[2], prv),
        remote(4, send.at[3], recv.at[3], nxt),
    ]

    row = lax.broadcasted_iota(jnp.int32, (NV * NV * ROWS, 1), 0)
    source = (row & (ROWS - 1)) * 32 + (row >> 4)
    column = lax.broadcasted_iota(jnp.int32, (NV * NV * ROWS, OWN * 32), 1)
    perm[...] = jnp.where(column == source, 1.0, 0.0).astype(BF16)
    vt[:, 8:, :] = jnp.zeros((NV, 8, 1024), F32)
    va[:, 8:, :] = jnp.zeros((NV, 8, 1024), F32)
    vfar[:, 8:, :] = jnp.zeros((NV, 8, 1024), F32)
    mpad[:, 16:, :] = jnp.zeros((OWN, 16, 1024), BF16)
    spread[:, :, 8:, :] = jnp.zeros((2, NV, 8, 256), F32)

    pl.semaphore_wait(barrier, 3)
    for copy in tan_sends:
        copy.start()

    for copy in first:
        copy.wait()
    order = order_ref[...]
    index = jnp.zeros((1, 128), F32)
    for k in range(NH):
        index = jnp.where(order == k, phase_ref[k].astype(F32), index)
    angle = (2.0 * math.pi / passages) * index
    cosine, sine = jnp.cos(angle), jnp.sin(angle)
    a1, a2 = a_ref[:FR], a_ref[FR:]
    both = jnp.concatenate([a1 * cosine + a2 * sine, a1 * cosine - a2 * sine], 0)
    rot = jnp.dot(both, f_ref[...], preferred_element_type=F32, precision=lax.Precision.HIGHEST)
    rot_lo, rot_up = [jnp.concatenate(split(rot[n * FR : (n + 1) * FR]), 0) for n in range(2)]

    for table, sel in ((lo_ref, sel_lo), (up_ref, sel_up)):
        for h in range(2):
            cells = lax.broadcasted_iota(jnp.int32, (512, 128), 0) + 512 * h
            hit = cells == table[:, 128 * h : 128 * h + 128]
            sel[h] = jnp.where(hit, 1.0, 0.0).astype(BF16)

    def regroup(src, dst):
        for t in range(OWN):
            mpad[t, 0:25, :] = src[t]
        for n in range(4):
            lanes = slice(256 * n, 256 * n + 256)
            part = mpad[:, :, lanes].reshape(OWN * 32, 256)
            dst[:, :, lanes] = dot(perm[...], part).reshape(NV * NV, ROWS, 256)

    def block(m, src, i, lanes, transposed):
        total = None
        for j in range(NV):
            e = j * NV + i if transposed else i * NV + j
            term = m[e, :, lanes] * src[j, :, lanes]
            total = term if total is None else total + term
        return total

    def faces(field_hi, field_lo, base):
        halves = jnp.concatenate([field_hi, field_lo], 0)
        for n, (sel, rotation) in enumerate(((sel_lo, rot_lo), (sel_up, rot_up))):
            picked = jnp.concatenate(
                [dot(halves[:, 512 * h : 512 * h + 512], sel[h]) for h in range(2)], 1
            ).astype(BF16)
            turned = dot(rotation, picked[: 2 * VR])
            total = turned[:FR] + turned[FR:] + dot(rotation[:FR], picked[2 * VR :])
            if base == 2:
                total = total * (bot_ref[...] if n == 0 else upw_ref[...])
            send[base + n] = total
            face_sends[base + n].start()

    def mixed(field_hi, field_lo):
        twice = dot(deriv_ref[...], field_hi)
        return twice[:VR] + twice[VR:] + dot(deriv_ref[:VR], field_lo)

    def field(own, far):
        return split(jnp.concatenate([own.reshape(VR, 1024), far.reshape(VR, 1024)], 0))

    for copy in tan_loads:
        copy.wait()
    for j in range(NV):
        vt[j, 0:OWN, :] = tan_own[j]
    for copy in tan_sends:
        copy.wait()
    for j in range(NV):
        vfar[j, 0:OWN, :] = tan_far[j]
    tan_hi, tan_lo = field(vt[...], vfar[...])
    faces(tan_hi, tan_lo, 0)

    pre_load.wait()
    regroup(pre, pt)
    for copy in adj_loads:
        copy.wait()
    for j in range(NV):
        va[j, 0:OWN, :] = adj_own[j]
    for n in range(8):
        for i in range(NV):
            vd[i, :, chunk(n)] = block(pt, va, i, chunk(n), True)
    send_dual.start()

    for copy in weights:
        copy.wait()
    deriv_load.wait()
    img[0] = mixed(tan_hi, tan_lo).reshape(NV, ROWS, 1024)
    jac_load.wait()
    regroup(jac, jt)
    lane = lax.broadcasted_iota(jnp.int32, (ROWS, 1024), 1)
    upwind = upwind_ref[...]

    send_dual.wait()
    dual_hi, dual_lo = field(vd[...], dual_far[...])
    faces(dual_hi, dual_lo, 2)

    for i in range(NV):
        before = jnp.where(lane == 0, 0.0, pltpu.roll(vt[i], 1, 1))
        img[0, i] = img[0, i] - upwind * before
    for n in range(8):
        for i in range(NV):
            img[0, i, :, chunk(n)] = img[0, i, :, chunk(n)] + block(jt, vt, i, chunk(n), False)

    img[1] = -mixed(dual_hi, dual_lo).reshape(NV, ROWS, 1024)
    for i in range(NV):
        after = jnp.where(lane == 1023, 0.0, pltpu.roll(upwind * vd[i], 1023, 1))
        img[1, i] = img[1, i] - after
    for n in range(8):
        for i in range(NV):
            img[1, i, :, chunk(n)] = img[1, i, :, chunk(n)] + block(jt, vd, i, chunk(n), True)

    def add_faces(base, scales):
        for n in range(2):
            for j in range(NV):
                got = recv[base + n, j * OWN : j * OWN + OWN, :]
                spread[n, j, 0:OWN, :] = got if scales is None else got * scales[n][...]
        pair = [jnp.concatenate(split(spread[n].reshape(VR, 256)), 0) for n in range(2)]
        for h in range(2):
            cells = slice(512 * h, 512 * h + 512)
            part = slice(128 * h, 128 * h + 128)
            total = dot_t(pair[0][:, part], sel_up[h]) + dot_t(pair[1][:, part], sel_lo[h])
            total = (total[:VR] + total[VR:]).reshape(NV, ROWS, 512)
            img[base // 2, :, :, cells] = img[base // 2, :, :, cells] - total

    for copy in face_sends[:2]:
        copy.wait()
    add_faces(0, (upw_ref, bot_ref))
    for n in range(8):
        for i in range(NV):
            tan_stage[i, :, chunk(n)] = block(pt, img.at[0], i, chunk(n), False)[:OWN]

    for copy in face_sends[2:]:
        copy.wait()
    add_faces(2, None)
    for n in range(8):
        adj_stage[:, :, chunk(n)] = img[1, :, 0:OWN, chunk(n)]


def finish(tan_ref, adj_ref, tan_out, adj_out, sems):
    stores = [
        pltpu.make_async_copy(
            src.at[:, :, 128 * n : 128 * n + 128], dst.at[:, :, n, 0, :], sems.at[m, n]
        )
        for m, (src, dst) in enumerate(((tan_ref, tan_out), (adj_ref, adj_out)))
        for n in range(8)
    ]
    for copy in stores:
        copy.start()
    for copy in stores:
        copy.wait()


def on_device(
    tangent_seed, adjoint_seed, jacobian, precond, upwind, up_weight, bottom_face_strength,
    up_cells, lo_cells, phase_index,
):
    passages = tangent_seed.shape[0] * lax.axis_size("blade")
    deriv, a, f, order = constants()
    own = (NV, OWN, 1024)
    field = (NV, ROWS, 1024)
    linear = (NV, OWN, 8, 1, 128)
    hbm = pl.BlockSpec(memory_space=pltpu.HBM)
    vmem = pl.BlockSpec(memory_space=pltpu.VMEM)
    staged = pl.pallas_call(
        functools.partial(kernel, passages),
        out_shape=(pltpu.VMEM(own, F32), pltpu.VMEM(own, F32)),
        in_specs=[hbm] * 14,
        out_specs=(vmem, vmem),
        scratch_shapes=[
            pltpu.VMEM((1, 1024), F32),
            pltpu.VMEM((1, 256), F32),
            pltpu.VMEM((1, 256), F32),
            pltpu.VMEM((1, 256), jnp.int32),
            pltpu.VMEM((1, 256), jnp.int32),
            pltpu.SMEM((NH,), jnp.int32),
            pltpu.VMEM(deriv.shape, BF16),
            pltpu.VMEM(a.shape, F32),
            pltpu.VMEM(f.shape, F32),
            pltpu.VMEM(order.shape, jnp.int32),
            pltpu.VMEM(own, F32),
            pltpu.VMEM(own, F32),
            pltpu.VMEM(own, F32),
            pltpu.VMEM((OWN, 25, 1024), BF16),
            pltpu.VMEM((OWN, 25, 1024), BF16),
            pltpu.VMEM((OWN, 32, 1024), BF16),
            pltpu.VMEM((NV * NV * ROWS, OWN * 32), BF16),
            pltpu.VMEM((25, ROWS, 1024), F32),
            pltpu.VMEM((25, ROWS, 1024), F32),
            pltpu.VMEM(field, F32),
            pltpu.VMEM(field, F32),
            pltpu.VMEM(field, F32),
            pltpu.VMEM(field, F32),
            pltpu.VMEM(field, F32),
            pltpu.VMEM((2, 512, 128), BF16),
            pltpu.VMEM((2, 512, 128), BF16),
            pltpu.VMEM((4, FR, 256), F32),
            pltpu.VMEM((4, FR, 256), F32),
            pltpu.VMEM((2, NV, ROWS, 256), F32),
            pltpu.VMEM((2,) + field, F32),
            pltpu.SemaphoreType.DMA((12,)),
            pltpu.SemaphoreType.DMA((8,)),
            pltpu.SemaphoreType.DMA((8,)),
            pltpu.SemaphoreType.DMA((8,)),
            pltpu.SemaphoreType.DMA((8,)),
            pltpu.SemaphoreType.DMA((5,)),
            pltpu.SemaphoreType.DMA((5,)),
        ],
        compiler_params=pltpu.CompilerParams(
            collective_id=0, has_side_effects=True, vmem_limit_bytes=VMEM_LIMIT
        ),
        name="harmonic_blade_row",
    )(
        tangent_seed.reshape(linear), adjoint_seed.reshape(linear), jacobian, precond,
        upwind, up_weight, bottom_face_strength,
        up_cells.reshape(1, -1), lo_cells.reshape(1, -1), phase_index,
        deriv, a, f, order,
    )
    tangent_out, adjoint_out = pl.pallas_call(
        finish,
        out_shape=(jax.ShapeDtypeStruct(linear, F32), jax.ShapeDtypeStruct(linear, F32)),
        in_specs=[vmem, vmem],
        out_specs=(hbm, hbm),
        scratch_shapes=[pltpu.SemaphoreType.DMA((2, 8))],
        compiler_params=pltpu.CompilerParams(vmem_limit_bytes=4 * 1024 * 1024),
        name="finish",
    )(*staged)
    return (tangent_out.reshape(tangent_seed.shape), adjoint_out.reshape(adjoint_seed.shape))


def solution(mesh):
    in_specs = (
        P("blade", None, "inst", None),
        P("blade", None, "inst", None),
        P("blade", "inst", None, None),
        P("blade", "inst", None, None),
        P("blade", None),
        P("blade", None),
        P("blade", None),
        P(),
        P(),
        P(),
    )
    out_specs = (P("blade", None, "inst", None), P("blade", None, "inst", None))
    return jax.shard_map(
        on_device, mesh=mesh, in_specs=in_specs, out_specs=out_specs, check_vma=False
    )
```
